32 devices in a mesh: stratum: 8 (over z, core), replica: 4 (over y, x).
Axes of the slice: x: 2, y: 2, z: 4, core: 2. Of those that a mesh axis runs over, the one named last changes fastest.
Arguments:
- user_factors: float32 [131072, 128], P(('stratum', 'replica')), may hold values from -1.8 to 1.8
- item_factors: float32 [32768, 128], P('stratum'), may hold values from -1.8 to 1.8
- ratings: bfloat16 [2, 8192, 128, 128], P(None, ('stratum', 'replica')), may hold values from -9 to 9
- user_tile: int32 [2, 8192], P(None, ('stratum', 'replica')), may hold values from 0 to 31, as said below
- item_tile: int32 [2, 8192], P(None, ('stratum', 'replica')), may hold values from 0 to 31, as said below
- live_count: int32 [2, 32], P(None, ('stratum', 'replica')), may hold values from 64 to 256, as said below
- partner: int32 [8], replicated, may hold values from 0 to 7, as said below
Outputs:
- user_out: float32 [131072, 128], P(('stratum', 'replica'))
- item_out: float32 [32768, 128], P('stratum')
The draws below stay inside these ranges and needn't reach their ends.
Inputs may be any that keep to these rules, and one draw needn't show every extreme that they name: partner[i] = i XOR m for one m from 4 to 7, the same for every i. `user_tile`: within one device and one sub-epoch, its 256 slots name distinct pairs of user tile and item tile. `item_tile`: paired with user_tile as stated there. `live_count`: in every sub-epoch some device has all 256 slots live.
All inputs are finite; a program needn't handle non-finite values.
Results may differ from the reference program's by a relative error of at most 0.0012.
Values sent between devices are 32-bit elements; how exact they have to be, the bound alone decides.
No kernel may reach another device: no remote copies, remote signals or barrier semaphores. Data moves between devices by JAX's collectives and lax.ppermute only.
A program may use at most 128 MiB of HBM per device.

```python
import jax
import jax.numpy as jnp
from jax import lax

RANK = 128
TILE = 128
USER_TILES = 32
ITEM_TILES = 32
TILE_SLOTS = 256
SUBEPOCHS = 2
USERS = 131072
ITEMS = 32768
TILES = 8192
N_STRATUM = 8
N_REPLICA = 4


def pick_slots(one_key):
    return jax.random.permutation(one_key, USER_TILES * ITEM_TILES)[:TILE_SLOTS]


def slot_pairs(key):
    base_key = jax.random.fold_in(key, 17)
    all_keys = jax.random.split(base_key, SUBEPOCHS * N_STRATUM * N_REPLICA)
    chosen = jax.vmap(pick_slots)(all_keys)
    return chosen.reshape(SUBEPOCHS, TILE_SLOTS * N_STRATUM * N_REPLICA).astype(jnp.int32)


def draw_user_tile(key, part):
    return (slot_pairs(key) // ITEM_TILES).astype(jnp.int32)


def draw_item_tile(key, part):
    return (slot_pairs(key) % ITEM_TILES).astype(jnp.int32)


def draw_live_count(key, part):
    devices_all = N_STRATUM * N_REPLICA
    lower_counts = jax.random.randint(jax.random.fold_in(key, 3), (SUBEPOCHS, devices_all), TILE_SLOTS // 4, TILE_SLOTS + 1)
    fullest = jax.random.randint(jax.random.fold_in(key, 5), (SUBEPOCHS, 1), 0, devices_all)
    positions = jnp.arange(devices_all, dtype=jnp.int32)[None, :]
    return jnp.where(positions == fullest, TILE_SLOTS, lower_counts).astype(jnp.int32)


def draw_partner(key, part):
    flip_mask = jax.random.randint(jax.random.fold_in(key, 9), (), N_STRATUM // 2, N_STRATUM)
    return jnp.bitwise_xor(jnp.arange(N_STRATUM, dtype=jnp.int32), flip_mask).astype(jnp.int32)


def levels(key, extent, pieces, smallest, top_value):
    level, own = 1.0, jax.random.fold_in(key, 6)
    for dim, parts in pieces:
        heights = jnp.exp(jax.random.uniform(jax.random.fold_in(own, dim), (parts,), jnp.float32, smallest / len(pieces), top_value / len(pieces)))
        level = level * jnp.repeat(heights, extent[dim] // parts).reshape([-1 if axis == dim else 1 for axis in range(len(extent))])
    return level


def scatter_about(key, extent, width, reach, pieces=(), kind=jnp.bfloat16):
    drawn = width * jax.random.normal(key, extent, jnp.float32)
    if pieces:
        drawn = drawn * levels(key, extent, pieces, -0.22, 0.18)
    return jnp.clip(drawn, -reach, reach).astype(kind)


def setup_inputs(seed: int = 0) -> dict:
    keys = jax.random.split(jax.random.key(seed), 8)
    return {
        "user_factors": scatter_about(keys[0], (USERS, RANK), 0.3, 1.8, ((0, 32),), jnp.float32),
        "item_factors": scatter_about(keys[1], (ITEMS, RANK), 0.3, 1.8, ((0, 8),), jnp.float32),
        "ratings": scatter_about(keys[2], (SUBEPOCHS, TILES, TILE, TILE), 1.5, 9.0, ((1, 32),)),
        "user_tile": draw_user_tile(jax.random.fold_in(keys[7], 71), 0),
        "item_tile": draw_item_tile(jax.random.fold_in(keys[7], 71), 0),
        "live_count": draw_live_count(jax.random.fold_in(keys[7], 71), 0),
        "partner": draw_partner(jax.random.fold_in(keys[7], 71), 0),
    }


LEARNING_RATE = 0.05
WEIGHT_DECAY = 0.05


def lowered(values):
    return lax.optimization_barrier(values.astype(jnp.bfloat16)).astype(jnp.float32)


def device_terms(user_rows, block_rows, rating_slots, user_index, item_index, slot_total):
    user_low = lowered(user_rows).reshape(USER_TILES, TILE, RANK)
    item_low = lowered(block_rows).reshape(ITEM_TILES, TILE, RANK)
    left_tiles = jnp.take(user_low, user_index, axis=0)
    right_tiles = jnp.take(item_low, item_index, axis=0)
    predicted = jnp.einsum("sik,sjk->sij", left_tiles, right_tiles)
    residual = lowered(rating_slots.astype(jnp.float32) - predicted)
    slot_user = jnp.einsum("sij,sjk->sik", residual, right_tiles)
    slot_item = jnp.einsum("sij,sik->sjk", residual, left_tiles)
    live_mask = (jnp.arange(TILE_SLOTS, dtype=jnp.int32) < slot_total).astype(jnp.float32)
    pick_user = (user_index[:, None] == jnp.arange(USER_TILES, dtype=jnp.int32)[None, :]).astype(jnp.float32) * live_mask[:, None]
    pick_item = (item_index[:, None] == jnp.arange(ITEM_TILES, dtype=jnp.int32)[None, :]).astype(jnp.float32) * live_mask[:, None]
    grad_user = jnp.einsum("sa,sik->aik", pick_user, slot_user, precision=lax.Precision.HIGHEST)
    grad_item = jnp.einsum("sa,sik->aik", pick_item, slot_item, precision=lax.Precision.HIGHEST)
    return (grad_user.reshape(USER_TILES * TILE, RANK), jnp.sum(pick_user, axis=0),
            grad_item.reshape(ITEM_TILES * TILE, RANK), jnp.sum(pick_item, axis=0))


def per_device(packed):
    return device_terms(*packed)


def reference(user_factors, item_factors, ratings, user_tile, item_tile, live_count, partner):
    devices_all = N_STRATUM * N_REPLICA
    user_rows = user_factors.reshape(devices_all, USER_TILES * TILE, RANK)
    blocks = item_factors.reshape(N_STRATUM, ITEM_TILES * TILE, RANK)
    for epoch_index in range(SUBEPOCHS):
        if epoch_index > 0:
            blocks = jnp.take(blocks, partner.astype(jnp.int32), axis=0)
        device_blocks = jnp.repeat(blocks, N_REPLICA, axis=0)
        grad_user, seen_user, grad_item, seen_item = lax.map(per_device, (
            user_rows, device_blocks,
            ratings[epoch_index].reshape(devices_all, TILE_SLOTS, TILE, TILE),
            user_tile[epoch_index].reshape(devices_all, TILE_SLOTS),
            item_tile[epoch_index].reshape(devices_all, TILE_SLOTS),
            live_count[epoch_index]))
        user_scale = jnp.repeat(jnp.maximum(seen_user, 1.0), TILE, axis=1)[:, :, None]
        user_rows = user_rows * (1.0 - LEARNING_RATE * WEIGHT_DECAY) + LEARNING_RATE * grad_user / user_scale
        stratum_grad = jnp.sum(grad_item.reshape(N_STRATUM, N_REPLICA, ITEM_TILES * TILE, RANK), axis=1)
        stratum_seen = jnp.sum(seen_item.reshape(N_STRATUM, N_REPLICA, ITEM_TILES), axis=1)
        item_scale = jnp.repeat(jnp.maximum(stratum_seen, 1.0), TILE, axis=1)[:, :, None]
        blocks = blocks * (1.0 - LEARNING_RATE * WEIGHT_DECAY) + LEARNING_RATE * stratum_grad / item_scale
    return user_rows.reshape(devices_all * USER_TILES * TILE, RANK), blocks.reshape(N_STRATUM * ITEM_TILES * TILE, RANK)
```

```python
import functools

import jax
import jax.numpy as jnp
from jax import lax
from jax.experimental import pallas as pl
from jax.experimental.pallas import tpu as pltpu
from jax.sharding import PartitionSpec as P

LEARNING_RATE = 0.05
WEIGHT_DECAY = 0.05
KEEP = 1.0 - LEARNING_RATE * WEIGHT_DECAY

TILE = 128
CHUNKS = 2
UNITS = 8
AHEAD = 4
RING = AHEAD + 1
FIELD = 6
COUNT_ROWS = 8
VMEM_BYTES = 24 << 20
SLOT_VMEM_BYTES = 44 << 20

CONTRACT_LAST = (((1,), (1,)), ((), ()))
VMEM = pl.BlockSpec(memory_space=pltpu.VMEM)
SMEM = pl.BlockSpec(memory_space=pltpu.SMEM)
ANY = pl.BlockSpec(memory_space=pl.ANY)
PARAMS = pltpu.CompilerParams(vmem_limit_bytes=VMEM_BYTES)


def up(value, unit):
    return (value + unit - 1) // unit * unit


class Layout:
    def __init__(self, users, items, slots, chunks, replicas):
        self.users, self.items, self.slots = users, items, slots
        self.chunks, self.replicas = chunks, replicas
        self.tiles = items // chunks
        self.share = self.tiles // replicas
        self.groups = chunks * users
        self.cap = slots + self.groups
        self.step = 2 * UNITS
        self.order_cols = up(self.cap, 128)
        self.group_cols = up(self.groups + 1, 128)
        self.item_cols = up(items, 128)
        self.base_at = self.order_cols
        self.count_at = self.base_at + self.group_cols
        self.seen_at = self.count_at + self.group_cols
        self.columns = self.seen_at + self.item_cols


def column(row, across):
    return jnp.broadcast_to(row, (across, row.shape[1])).T


def low_tiles(rows, low_ref, lowt_ref, a):
    low_ref[a] = rows.astype(jnp.bfloat16)
    lowt_ref[a] = rows.T.astype(jnp.bfloat16)


def prepare_kernel(lay, epochs, user_ref, item_ref, live_ref, rows_ref, table_ref, low_ref, lowt_ref):
    def iota(shape, axis):
        return lax.broadcasted_iota(jnp.int32, shape, axis)

    def total(mask, values=1):
        return jnp.sum(jnp.where(mask, values, 0), axis=0, keepdims=True)

    n, groups = lay.slots, lay.group_cols
    for e in range(epochs):
        user, item = user_ref[e : e + 1, :], item_ref[e : e + 1, :]
        live = iota((1, n), 1) < live_ref[e : e + 1, :]
        group = jnp.where(live, item // lay.tiles * lay.users + user, lay.groups)
        packed = user + (item << FIELD) + (iota((1, n), 1) << 2 * FIELD)
        same = column(group, n) == group
        rank = total(same & (iota((n, n), 0) < iota((n, n), 1)))
        count = total(column(group, groups) == iota((n, groups), 1))
        padded = (count + 1) // 2 * 2
        base = total(iota((groups, groups), 0) < iota((groups, groups), 1), column(padded, groups))
        place = rank + total(iota((groups, n), 0) == group, column(base, n))
        place = jnp.where(live, place, -1)
        order = total(column(place, lay.order_cols) == iota((n, lay.order_cols), 1), column(packed, lay.order_cols))
        every = iota((1, groups), 1)
        spare = jnp.where((count % 2 == 1) & (every < lay.groups), base + count, -1)
        order += total(
            column(spare, lay.order_cols) == iota((groups, lay.order_cols), 1),
            column(every % lay.users + (lay.items << FIELD), lay.order_cols),
        )
        tile = jnp.where(live, item, lay.items)
        seen = total(column(tile, lay.item_cols) == iota((n, lay.item_cols), 1))
        table_ref[e : e + 1, 0 : lay.base_at] = order
        table_ref[e : e + 1, lay.base_at : lay.count_at] = base
        table_ref[e : e + 1, lay.count_at : lay.seen_at] = count
        table_ref[e : e + 1, lay.seen_at : lay.columns] = seen

    def lower(a, _):
        low_tiles(rows_ref[pl.ds(pl.multiple_of(a * TILE, TILE), TILE), :], low_ref, lowt_ref, a)
        return 0

    lax.fori_loop(0, lay.users, lower, 0, unroll=4)
    low_ref[lay.users] = jnp.zeros((TILE, TILE), jnp.bfloat16)
    lowt_ref[lay.users] = jnp.zeros((TILE, TILE), jnp.bfloat16)


def low_shape(lay):
    return jax.ShapeDtypeStruct((lay.users + 1, TILE, TILE), jnp.bfloat16)


def prepare(lay, user_tile, item_tile, live_count, user_rows):
    epochs = user_tile.shape[0]
    return pl.pallas_call(
        functools.partial(prepare_kernel, lay, epochs),
        out_shape=[jax.ShapeDtypeStruct((epochs, lay.columns), jnp.int32), low_shape(lay), low_shape(lay)],
        in_specs=[VMEM] * 4,
        out_specs=[VMEM] * 3,
        compiler_params=PARAMS,
        name="prepare",
    )(user_tile, item_tile, live_count, user_rows)


def slots_kernel(lay, epoch, chunk, pieces_in, table_ref, me_ref, ratings_ref, low_ref, lowt_ref, *refs):
    block_refs, refs = refs[:pieces_in], refs[pieces_in:]
    user_grad, piece_refs = refs[0], refs[1 : 1 + lay.replicas]
    buf, sems, item_low, item_grad = refs[1 + lay.replicas :]
    me = me_ref[0]
    begin = table_ref[epoch, lay.base_at + chunk * lay.users]
    end = table_ref[epoch, lay.base_at + (chunk + 1) * lay.users]
    steps = (end - begin + lay.step - 1) // lay.step
    zero = jnp.zeros((TILE, TILE), jnp.float32)

    def fetch(g):
        for s in range(lay.step):
            packed = table_ref[epoch, jnp.minimum(begin + g * lay.step + s, lay.cap - 1)]
            slot = lax.shift_right_logical(packed, 2 * FIELD)
            pltpu.make_async_copy(ratings_ref.at[epoch, slot], buf.at[g % RING, s], sems.at[g % RING]).start()

    def fetch_first(g, _):
        fetch(g)
        return 0

    lax.fori_loop(0, jnp.minimum(AHEAD, steps), fetch_first, 0)

    for j in range(lay.tiles):
        item_grad[j] = zero
    if pieces_in == 1:
        for j in range(lay.tiles):
            item_low[j] = block_refs[0][j * TILE : (j + 1) * TILE, :].astype(jnp.bfloat16)
    else:
        for k in range(lay.replicas):
            first = lax.bitwise_xor(me, k) * lay.share
            for j in range(lay.share):
                item_low[first + j] = block_refs[k][j * TILE : (j + 1) * TILE, :].astype(jnp.bfloat16)
    item_low[lay.tiles] = jnp.zeros((TILE, TILE), jnp.bfloat16)

    def clear(a, _):
        user_grad[a] = zero
        return 0

    lax.fori_loop(0, lay.users, clear, 0, unroll=4)

    def step(g, _):
        @pl.when(g + AHEAD < steps)
        def _():
            fetch(g + AHEAD)

        first = begin + g * lay.step
        here = buf.at[g % RING]
        pltpu.make_async_copy(ratings_ref.at[epoch, pl.ds(0, lay.step)], here, sems.at[g % RING]).wait()
        units = []
        for n in range(UNITS):
            items = []
            for s in range(2):
                place = first + 2 * n + s
                packed = table_ref[epoch, jnp.minimum(place, lay.cap - 1)]
                item = lax.shift_right_logical(packed, FIELD) % (1 << FIELD) - chunk * lay.tiles
                items.append(jnp.where((place < end) & (item >= 0) & (item < lay.tiles), item, lay.tiles))
            user = jnp.where(place < end, packed % (1 << FIELD), lay.users)
            right = jnp.concatenate([item_low[b] for b in items], axis=0)
            predicted = lax.dot_general(low_ref[user], right, CONTRACT_LAST, preferred_element_type=jnp.float32)
            rating = jnp.concatenate([buf[g % RING, 2 * n + s] for s in range(2)], axis=1)
            residual = (rating.astype(jnp.float32) - predicted).astype(jnp.bfloat16)
            units.append((user, items, right, residual))
        for user, items, right, residual in units:
            user_grad[user] += jnp.dot(residual, right, preferred_element_type=jnp.float32)
            part = jnp.dot(lowt_ref[user], residual, preferred_element_type=jnp.float32)
            for s in range(2):
                item_grad[items[s]] += part[:, s * TILE : (s + 1) * TILE]
        return 0

    lax.fori_loop(0, steps, step, 0)

    row = lax.broadcasted_iota(jnp.int32, (COUNT_ROWS, TILE), 0)
    for k in range(lay.replicas):
        first = lax.bitwise_xor(me, k) * lay.share
        counts = jnp.zeros((COUNT_ROWS, TILE), jnp.int32)
        for j in range(lay.share):
            piece_refs[k][j * TILE : (j + 1) * TILE, :] = item_grad[first + j].T
            seen = table_ref[epoch, lay.seen_at + chunk * lay.tiles + first + j]
            counts = jnp.where(row == j, seen, counts)
        piece_refs[k][lay.share * TILE :, :] = counts.astype(jnp.float32)


def slot_terms(lay, epoch, chunk, table, me, ratings, low, lowt, blocks):
    if len(blocks) == 1:
        block_specs = [pl.BlockSpec((lay.tiles * TILE, TILE), lambda i: (chunk, 0))]
    else:
        block_specs = [VMEM] * len(blocks)
    piece = jax.ShapeDtypeStruct((lay.share * TILE + COUNT_ROWS, TILE), jnp.float32)
    user_grad = jax.ShapeDtypeStruct((lay.users + 1, TILE, TILE), jnp.float32)
    live = lay.slots // lay.chunks
    out = pl.pallas_call(
        functools.partial(slots_kernel, lay, epoch, chunk, len(blocks)),
        grid=(1,),
        out_shape=[user_grad] + [piece] * lay.replicas,
        in_specs=[SMEM, SMEM, ANY, VMEM, VMEM] + block_specs,
        out_specs=[VMEM] * (1 + lay.replicas),
        scratch_shapes=[
            pltpu.VMEM((RING, lay.step, TILE, TILE), jnp.bfloat16),
            pltpu.SemaphoreType.DMA((RING,)),
            pltpu.VMEM((lay.tiles + 1, TILE, TILE), jnp.bfloat16),
            pltpu.VMEM((lay.tiles + 1, TILE, TILE), jnp.float32),
        ],
        cost_estimate=pl.CostEstimate(
            flops=6 * live * TILE**3 * 4, bytes_accessed=live * TILE * TILE * 2, transcendentals=0
        ),
        compiler_params=pltpu.CompilerParams(vmem_limit_bytes=SLOT_VMEM_BYTES),
        name="slots",
    )(table, me, ratings, low, lowt, *blocks)
    return out[0], list(out[1:])


def user_kernel(lay, epoch, last, table_ref, rows_ref, *refs):
    grads, refs = refs[: lay.chunks], refs[lay.chunks :]

    def one(a, _):
        seen = sum(table_ref[epoch, lay.count_at + c * lay.users + a] for c in range(lay.chunks))
        seen = jnp.maximum(jnp.broadcast_to(seen, (1, TILE)).astype(jnp.float32), 1.0)
        at = pl.ds(pl.multiple_of(a * TILE, TILE), TILE)
        grad = sum(grad_ref[a] for grad_ref in grads)
        rows = rows_ref[at, :] * KEEP + grad * (LEARNING_RATE / seen)
        refs[0][at, :] = rows
        if not last:
            low_tiles(rows, refs[1], refs[2], a)
        return 0

    lax.fori_loop(0, lay.users, one, 0, unroll=4)
    if not last:
        refs[1][lay.users] = jnp.zeros((TILE, TILE), jnp.bfloat16)
        refs[2][lay.users] = jnp.zeros((TILE, TILE), jnp.bfloat16)


def user_step(lay, epoch, last, table, rows, grads):
    out_shape = [jax.ShapeDtypeStruct(rows.shape, jnp.float32)]
    if not last:
        out_shape += [low_shape(lay)] * 2
    return pl.pallas_call(
        functools.partial(user_kernel, lay, epoch, last),
        out_shape=out_shape,
        in_specs=[SMEM] + [VMEM] * (1 + len(grads)),
        out_specs=[VMEM] * len(out_shape),
        compiler_params=PARAMS,
        name="users",
    )(table, rows, *grads)


def item_kernel(lay, me_ref, old_ref, *refs):
    parts, out_ref = refs[:-1], refs[-1]
    for j in range(lay.share):
        at = slice(j * TILE, (j + 1) * TILE)
        row = lay.share * TILE + j
        seen = jnp.maximum(sum(part[row : row + 1, :] for part in parts), 1.0)
        grad = sum(part[at, :] for part in parts)
        out_ref[at, :] = old_ref[at, :] * KEEP + grad * (LEARNING_RATE / seen)


def item_step(lay, chunk, me, old, parts):
    rows = lay.share * TILE
    whole = old.shape[0] != rows
    grid_spec = pltpu.PrefetchScalarGridSpec(
        num_scalar_prefetch=1,
        grid=(1,),
        in_specs=[
            pl.BlockSpec((rows, TILE), lambda i, me: (chunk * lay.replicas + me[0] if whole else 0, 0))
        ]
        + [VMEM] * len(parts),
        out_specs=pl.BlockSpec((rows, TILE), lambda i, me: (0, 0)),
    )
    return pl.pallas_call(
        functools.partial(item_kernel, lay),
        grid_spec=grid_spec,
        out_shape=jax.ShapeDtypeStruct((rows, TILE), jnp.float32),
        compiler_params=PARAMS,
        name="items",
    )(me, old, *parts)


def assemble_kernel(lay, me_ref, *refs):
    pieces, out_ref, sems = refs[:-2], refs[-2], refs[-1]
    rows = lay.share * TILE
    copies = []
    for c in range(lay.chunks):
        for k in range(lay.replicas):
            first = (c * lay.replicas + lax.bitwise_xor(me_ref[0], k)) * rows
            at = pl.ds(pl.multiple_of(first, TILE), rows)
            n = c * lay.replicas + k
            copies.append(pltpu.make_async_copy(pieces[n], out_ref.at[at, :], sems.at[n]))
            copies[-1].start()
    for copy in copies:
        copy.wait()


def assemble(lay, me, pieces):
    return pl.pallas_call(
        functools.partial(assemble_kernel, lay),
        out_shape=jax.ShapeDtypeStruct((lay.items * TILE, TILE), jnp.float32),
        in_specs=[SMEM] + [VMEM] * len(pieces),
        out_specs=ANY,
        scratch_shapes=[pltpu.SemaphoreType.DMA((len(pieces),))],
        compiler_params=PARAMS,
        name="assemble",
    )(me, *pieces)


def swap(value, axis, mask):
    return lax.ppermute(value, axis, [(i, i ^ mask) for i in range(lax.axis_size(axis))])


def gather_sum(pieces, bits):
    held = {k: [piece] for k, piece in enumerate(pieces)}
    for bit in bits:
        for k in [k for k in held if k & bit]:
            sent = held.pop(k)
            held[k ^ bit] = held[k ^ bit] + [swap(functools.reduce(jnp.add, sent), "replica", bit)]
    return held[0]


def spread(own, bits):
    held = {0: own}
    for bit in reversed(bits):
        for k in list(held):
            held[k ^ bit] = swap(held[k], "replica", bit)
    return [held[k] for k in sorted(held)]


def steps(flip, lay, user_factors, item_factors, ratings, user_tile, item_tile, live_count):
    me = lax.axis_index("replica").astype(jnp.int32).reshape(1)
    levels = lay.replicas.bit_length() - 1
    bits = [[1 << (c + i) % levels for i in range(levels)] for c in range(lay.chunks)]
    epochs = ratings.shape[0]
    rows = user_factors
    table, low, lowt = prepare(lay, user_tile, item_tile, live_count, rows)
    blocks = [[item_factors]] * lay.chunks
    for e in range(epochs):
        last = e + 1 == epochs
        grads, parts = [], []
        for c in range(lay.chunks):
            grad, pieces = slot_terms(lay, e, c, table, me, ratings, low, lowt, blocks[c])
            grads.append(grad)
            parts.append(gather_sum(pieces, bits[c]))
        if last:
            (rows,) = user_step(lay, e, last, table, rows, grads)
        else:
            rows, low, lowt = user_step(lay, e, last, table, rows, grads)
        fresh = []
        for c in range(lay.chunks):
            own = item_step(lay, c, me, blocks[c][0], parts[c])
            if not last:
                own = swap(own, "stratum", flip)
            fresh.append(spread(own, bits[c]))
        blocks = fresh
    return rows, assemble(lay, me, [piece for chunk in blocks for piece in chunk])


def local(user_factors, item_factors, ratings, user_tile, item_tile, live_count, partner):
    users, items = user_factors.shape[0] // TILE, item_factors.shape[0] // TILE
    replicas, strata = lax.axis_size("replica"), lax.axis_size("stratum")
    lay = Layout(users, items, ratings.shape[1], CHUNKS, replicas)
    branches = [functools.partial(steps, flip, lay) for flip in range(strata // 2, strata)]
    args = (user_factors, item_factors, ratings, user_tile, item_tile, live_count)
    return lax.switch(partner[0] - strata // 2, branches, *args)


def solution(mesh):
    split = P(("stratum", "replica"), None)
    return jax.shard_map(
        local,
        mesh=mesh,
        in_specs=(
            split,
            P("stratum", None),
            P(None, ("stratum", "replica"), None, None),
            P(None, ("stratum", "replica")),
            P(None, ("stratum", "replica")),
            P(None, ("stratum", "replica")),
            P(),
        ),
        out_specs=(split, P("stratum", None)),
        check_vma=False,
    )
```

```python
import functools

import jax
import jax.numpy as jnp
from jax import lax
from jax.experimental import pallas as pl
from jax.experimental.pallas import tpu as pltpu
from jax.sharding import PartitionSpec as P

LEARNING_RATE = 0.05
WEIGHT_DECAY = 0.05
KEEP = 1.0 - LEARNING_RATE * WEIGHT_DECAY

TILE = 128
SPLIT = (1, 1)
LANES = (1, 2)
DIRECT_SUM = ((1, 1), (0, 0))
DIRECT_SPREAD = ((1, 1), (0, 0))
UNITS = 8
STEP = 2 * UNITS
AHEAD = 3
RING = 4
FIELD = 6
COUNT_ROWS = 8
VMEM_BYTES = 24 << 20
SLOT_VMEM_BYTES = 44 << 20

CONTRACT_LAST = (((1,), (1,)), ((), ()))
VMEM = pl.BlockSpec(memory_space=pltpu.VMEM)
SMEM = pl.BlockSpec(memory_space=pltpu.SMEM)
ANY = pl.BlockSpec(memory_space=pl.ANY)
PARAMS = pltpu.CompilerParams(vmem_limit_bytes=VMEM_BYTES)


def up(value, unit):
    return (value + unit - 1) // unit * unit


class Lane:
    def __init__(self, chunk_first, share, lane, lanes, replicas):
        self.chunk_first, self.share, self.replicas = chunk_first, share, replicas
        self.tiles = share // lanes
        self.skip = lane * self.tiles
        self.rows = self.tiles * TILE
        self.sent = self.rows + COUNT_ROWS
        levels = replicas.bit_length() - 1
        self.bits = [1 << (lane + i) % levels for i in range(levels)]

    def arrays(self, direct):
        if direct:
            return [[k] for k in range(self.replicas)]
        order = sorted(range(self.replicas), key=lambda k: [k & bit for bit in self.bits])
        return [order[: self.replicas // 2], order[self.replicas // 2 :]]

    def first(self, me, k):
        return lax.bitwise_xor(me, k) * self.share + self.skip


class Layout:
    def __init__(self, users, items, slots, replicas):
        self.users, self.items, self.slots, self.replicas = users, items, slots, replicas
        self.tiles = [items * part // sum(SPLIT) for part in SPLIT]
        self.firsts = [sum(self.tiles[:c]) for c in range(len(SPLIT))]
        self.chunks = len(SPLIT)
        self.lanes = []
        for wanted in LANES:
            self.lanes.append([])
            for c in range(self.chunks):
                share = self.tiles[c] // replicas
                lanes = wanted if share % wanted == 0 else 1
                self.lanes[-1].append([Lane(self.firsts[c], share, n, lanes, replicas) for n in range(lanes)])
        self.groups = self.chunks * users
        self.group_cols = up(self.groups + 1, 128)
        self.steps = up((slots + self.groups) // STEP + self.chunks + AHEAD + 1, 8)
        self.start_at = self.steps
        self.count_at = self.start_at + self.group_cols // 128
        self.seen_at = self.count_at + 1
        self.table_rows = up(self.seen_at + 1, 8)

    def start(self, table_ref, epoch, chunk):
        at = chunk * self.users
        row = lax.shift_right_logical(at, 7)
        return table_ref[epoch * self.table_rows + self.start_at + row, lax.bitwise_and(at, 127)]


def column(row, across):
    return jnp.broadcast_to(row, (across, row.shape[1])).T


def low_tiles(rows, low_ref, lowt_ref, a):
    low_ref[a] = rows.astype(jnp.bfloat16)
    lowt_ref[a] = rows.T.astype(jnp.bfloat16)


def slot_table(lay, user, item, live):
    def iota(shape, axis):
        return lax.broadcasted_iota(jnp.int32, shape, axis)

    def total(mask, values=1):
        return jnp.sum(jnp.where(mask, values, 0), axis=0, keepdims=True)

    n, groups, users = lay.slots, lay.group_cols, lay.users
    chunk = sum((item >= first).astype(jnp.int32) for first in lay.firsts[1:]) + jnp.zeros_like(item)
    local = item - sum(jnp.where(chunk == c, first, 0) for c, first in enumerate(lay.firsts))
    group = jnp.where(live, chunk * users + user, lay.groups)
    packed = user + (local << FIELD) + (iota((1, n), 1) << 2 * FIELD)
    same = column(group, n) == group
    rank = total(same & (iota((n, n), 0) < iota((n, n), 1)))
    count = total(column(group, groups) == iota((n, groups), 1))
    padded = column((count + 1) // 2 * 2, groups)
    above, here = iota((groups, groups), 0), iota((groups, groups), 1)
    inside = total((above < here) & (above // users == here // users), padded)
    steps = (total(above // users == here // users, padded) + STEP - 1) // STEP
    start = total((above % users == 0) & (above // users < here // users), column(steps, groups))
    base = start * STEP + inside
    place = rank + total(iota((groups, n), 0) == group, column(base, n))
    place = jnp.where(live, place, -1)
    every = iota((1, groups), 1)
    spare = jnp.where((count % 2 == 1) & (every < lay.groups), base + count, -1)
    pad = sum(jnp.where(every // users == c, tiles, 0) for c, tiles in enumerate(lay.tiles))
    cols = lay.steps * STEP
    cols = up(cols, 128)
    order = total(column(place, cols) == iota((n, cols), 1), column(packed - users, cols))
    order += total(column(spare, cols) == iota((groups, cols), 1), column(every % users - users + (pad << FIELD), cols))
    order += users
    seen_user = total(column(jnp.where(live, user, -1), 128) == iota((n, 128), 1))
    seen_item = total(column(jnp.where(live, item, -1), 128) == iota((n, 128), 1))
    return order, start, seen_user, seen_item


def prepare_kernel(lay, epochs, user_ref, item_ref, live_ref, rows_hbm, table_ref, low_ref, lowt_ref, rows_ref, sems):
    parts = sems.shape[0]
    height = rows_ref.shape[0] // parts
    copies = []
    for p in range(parts):
        at = pl.ds(p * height, height)
        copies.append(pltpu.make_async_copy(rows_hbm.at[at, :], rows_ref.at[at, :], sems.at[p]))
        copies[-1].start()
    for e in range(epochs):
        live = lax.broadcasted_iota(jnp.int32, (1, lay.slots), 1) < live_ref[:, e : e + 1]
        order, start, seen_user, seen_item = slot_table(lay, user_ref[e : e + 1, :], item_ref[e : e + 1, :], live)
        top = e * lay.table_rows
        mask = (1 << FIELD) - 1
        for at, values in ((0, order >> 2 * FIELD), (STEP, order & mask), (2 * STEP, (order >> FIELD) & mask)):
            for g in range(lay.steps):
                table_ref[top + g : top + g + 1, at : at + STEP] = values[:, g * STEP : (g + 1) * STEP]
        for n in range(lay.group_cols // 128):
            table_ref[top + lay.start_at + n : top + lay.start_at + n + 1, :] = start[:, n * 128 : (n + 1) * 128]
        table_ref[top + lay.count_at : top + lay.count_at + 1, :] = seen_user
        table_ref[top + lay.seen_at : top + lay.seen_at + 1, :] = seen_item
    low_ref[lay.users] = jnp.zeros((TILE, TILE), jnp.bfloat16)
    lowt_ref[lay.users] = jnp.zeros((TILE, TILE), jnp.bfloat16)
    share = lay.users // parts
    for p in range(parts):
        copies[p].wait()

        def lower(i, _, p=p):
            a = p * share + i
            low_tiles(rows_ref[pl.ds(pl.multiple_of(a * TILE, TILE), TILE), :], low_ref, lowt_ref, a)
            return 0

        lax.fori_loop(0, share, lower, 0, unroll=4)


def low_shape(lay):
    return jax.ShapeDtypeStruct((lay.users + 1, TILE, TILE), jnp.bfloat16)


def prepare(lay, user_tile, item_tile, live_count, user_rows):
    epochs = user_tile.shape[0]
    parts = 4
    return pl.pallas_call(
        functools.partial(prepare_kernel, lay, epochs),
        out_shape=[
            jax.ShapeDtypeStruct((epochs * lay.table_rows, 128), jnp.int32),
            low_shape(lay),
            low_shape(lay),
        ],
        in_specs=[VMEM, VMEM, VMEM, ANY],
        out_specs=[VMEM] * 3,
        scratch_shapes=[pltpu.VMEM(user_rows.shape, jnp.float32), pltpu.SemaphoreType.DMA((parts,))],
        compiler_params=PARAMS,
        name="prepare",
    )(user_tile, item_tile, live_count, user_rows)


def slots_kernel(
    lay, sources, targets, tiles, table_ref, me_ref, where_ref, ratings_ref, low_ref, lowt_ref, *refs
):
    count_in = sum(len(arrays) for _, arrays in sources) if sources else 1
    count_out = sum(len(arrays) for _, arrays in targets)
    block_refs, refs = refs[:count_in], refs[count_in:]
    user_grad, piece_refs = refs[0], refs[1 : 1 + count_out]
    buf, sems, item_low, item_grad = refs[1 + count_out :]
    me, epoch, chunk, chunk_first = me_ref[0], where_ref[0], where_ref[1], where_ref[2]
    top = epoch * lay.table_rows + lay.start(table_ref, epoch, chunk)
    steps = lay.start(table_ref, epoch, chunk + 1) - lay.start(table_ref, epoch, chunk)
    zero = jnp.zeros((TILE, TILE), jnp.float32)

    def fetch(g):
        ring = lax.bitwise_and(g, RING - 1)
        for s in range(STEP):
            slot = table_ref[top + g, s]
            pltpu.make_async_copy(ratings_ref.at[epoch, slot], buf.at[ring, s], sems.at[ring]).start()

    def land(g):
        ring = lax.bitwise_and(g, RING - 1)
        pltpu.make_async_copy(ratings_ref.at[epoch, pl.ds(0, STEP)], buf.at[ring], sems.at[ring]).wait()

    def fetch_first(g, _):
        fetch(g)
        return 0

    lax.fori_loop(0, AHEAD, fetch_first, 0)

    if sources:
        inputs = iter(block_refs)
        for lane, arrays in sources:
            for pieces in arrays:
                block = next(inputs)
                for n, k in enumerate(pieces):
                    first = lane.first(me, k)
                    for j in range(lane.tiles):
                        at = n * lane.rows + j * TILE
                        item_low[first + j] = block[at : at + TILE, :].astype(jnp.bfloat16)
    else:


        def lower(j, _):
            at = pl.ds(pl.multiple_of((chunk_first + j) * TILE, TILE), TILE)
            item_low[j] = block_refs[0][at, :].astype(jnp.bfloat16)
            return 0

        lax.fori_loop(0, tiles, lower, 0, unroll=4)
    item_low[tiles] = jnp.zeros((TILE, TILE), jnp.bfloat16)

    def clear_item(a, _):
        item_grad[a] = zero
        return 0

    def clear_user(a, _):
        user_grad[a] = zero
        return 0

    lax.fori_loop(0, tiles, clear_item, 0, unroll=4)
    lax.fori_loop(0, lay.users, clear_user, 0, unroll=4)

    def step(g, _):
        land(g)
        fetch(g + AHEAD)
        ring = lax.bitwise_and(g, RING - 1)
        units = []
        for n in range(UNITS):
            user = table_ref[top + g, STEP + 2 * n]
            items = [table_ref[top + g, 2 * STEP + 2 * n + s] for s in range(2)]
            right = jnp.concatenate([item_low[b] for b in items], axis=0)
            predicted = lax.dot_general(low_ref[user], right, CONTRACT_LAST, preferred_element_type=jnp.float32)
            rating = jnp.concatenate([buf[ring, 2 * n + s] for s in range(2)], axis=1)
            residual = (rating.astype(jnp.float32) - predicted).astype(jnp.bfloat16)
            units.append((user, items, right, residual))
        for user, items, right, residual in units:
            user_grad[user] += jnp.dot(residual, right, preferred_element_type=jnp.float32)
            part = jnp.dot(lowt_ref[user], residual, preferred_element_type=jnp.float32)
            for s in range(2):
                item_grad[items[s]] += part[:, s * TILE : (s + 1) * TILE]
        return 0

    lax.fori_loop(0, steps, step, 0)

    def turn(j, _):
        item_grad[j] = item_grad[j].T
        return 0

    lax.fori_loop(0, tiles, turn, 0, unroll=2)
    row = lax.broadcasted_iota(jnp.int32, (COUNT_ROWS, TILE), 0)
    outputs = iter(piece_refs)
    for lane, arrays in targets:
        for pieces in arrays:
            out = next(outputs)
            for n, k in enumerate(pieces):
                first = lane.first(me, k)
                counts = jnp.zeros((COUNT_ROWS, TILE), jnp.int32)
                for j in range(lane.tiles):
                    at = n * lane.sent + j * TILE
                    out[at : at + TILE, :] = item_grad[first + j]
                    seen = table_ref[epoch * lay.table_rows + lay.seen_at, chunk_first + first + j]
                    counts = jnp.where(row == j, seen, counts)
                at = n * lane.sent + lane.rows
                out[at : at + COUNT_ROWS, :] = counts.astype(jnp.float32)

    def drain(g, _):
        land(steps + g)
        return 0

    lax.fori_loop(0, AHEAD, drain, 0)


def routes(lay, direct, epoch, chunk):
    return [(lane, lane.arrays(direct[epoch][chunk])) for lane in lay.lanes[epoch][chunk]]


def slot_terms(lay, epoch, chunk, table, me, ratings, low, lowt, blocks):
    sources = routes(lay, DIRECT_SPREAD, epoch - 1, chunk) if epoch else None
    targets = routes(lay, DIRECT_SUM, epoch, chunk)
    pieces = [
        jax.ShapeDtypeStruct((len(held) * lane.sent, TILE), jnp.float32)
        for lane, arrays in targets
        for held in arrays
    ]
    user_grad = jax.ShapeDtypeStruct((lay.users + 1, TILE, TILE), jnp.float32)
    live = lay.slots // lay.chunks
    where = jnp.array([epoch, chunk, lay.firsts[chunk]], jnp.int32)
    out = pl.pallas_call(
        functools.partial(slots_kernel, lay, sources, targets, lay.tiles[chunk]),
        out_shape=[user_grad] + pieces,
        in_specs=[SMEM, SMEM, SMEM, ANY, VMEM, VMEM] + [VMEM] * len(blocks),
        out_specs=[VMEM] * (1 + len(pieces)),
        scratch_shapes=[
            pltpu.VMEM((RING, STEP, TILE, TILE), jnp.bfloat16),
            pltpu.SemaphoreType.DMA((RING,)),
            pltpu.VMEM((lay.tiles[chunk] + 1, TILE, TILE), jnp.bfloat16),
            pltpu.VMEM((lay.tiles[chunk] + 1, TILE, TILE), jnp.float32),
        ],
        cost_estimate=pl.CostEstimate(
            flops=6 * live * TILE**3 * 4, bytes_accessed=live * TILE * TILE * 2, transcendentals=0
        ),
        compiler_params=pltpu.CompilerParams(vmem_limit_bytes=SLOT_VMEM_BYTES),
        name="slots",
    )(table, me, where, ratings, low, lowt, *blocks)
    parts = iter(out[1:])
    return out[0], [[next(parts) for _ in arrays] for _, arrays in targets]


def user_kernel(lay, epoch, last, table_ref, rows_ref, *refs):
    grads, refs = refs[: lay.chunks], refs[lay.chunks :]

    def one(a, _):
        seen = table_ref[epoch * lay.table_rows + lay.count_at, a]
        seen = jnp.maximum(jnp.broadcast_to(seen, (1, TILE)).astype(jnp.float32), 1.0)
        at = pl.ds(pl.multiple_of(a * TILE, TILE), TILE)
        grad = sum(grad_ref[a] for grad_ref in grads)
        rows = rows_ref[at, :] * KEEP + grad * (LEARNING_RATE / seen)
        refs[0][at, :] = rows
        if not last:
            low_tiles(rows, refs[1], refs[2], a)
        return 0

    lax.fori_loop(0, lay.users, one, 0, unroll=4)
    if not last:
        refs[1][lay.users] = jnp.zeros((TILE, TILE), jnp.bfloat16)
        refs[2][lay.users] = jnp.zeros((TILE, TILE), jnp.bfloat16)


def user_step(lay, epoch, last, table, rows, grads):
    out_shape = [jax.ShapeDtypeStruct(rows.shape, jnp.float32)]
    if not last:
        out_shape += [low_shape(lay)] * 2
    return pl.pallas_call(
        functools.partial(user_kernel, lay, epoch, last),
        out_shape=out_shape,
        in_specs=[SMEM] + [VMEM] * (1 + len(grads)),
        out_specs=[VMEM] * len(out_shape),
        compiler_params=PARAMS,
        name="users",
    )(table, rows, *grads)


def item_kernel(lane, whole, skip, me_ref, old_ref, *refs):
    parts, out_ref = refs[:-1], refs[-1]
    first = lane.chunk_first + lane.first(me_ref[0], 0) if whole else skip
    for j in range(lane.tiles):
        at = slice(j * TILE, (j + 1) * TILE)
        from_tile = (first + j) * TILE
        old = old_ref[pl.ds(pl.multiple_of(from_tile, TILE) if whole else from_tile, TILE), :]
        row = lane.rows + j
        seen = jnp.maximum(sum(part[row : row + 1, :] for part in parts), 1.0)
        grad = sum(part[at, :] for part in parts)
        out_ref[at, :] = old * KEEP + grad * (LEARNING_RATE / seen)


def item_step(lane, whole, skip, me, old, parts):
    return pl.pallas_call(
        functools.partial(item_kernel, lane, whole, skip),
        out_shape=jax.ShapeDtypeStruct((lane.rows, TILE), jnp.float32),
        in_specs=[SMEM] + [VMEM] * (1 + len(parts)),
        out_specs=VMEM,
        compiler_params=PARAMS,
        name="items",
    )(me, old, *parts)


def assemble_kernel(lay, sources, me_ref, *refs):
    arrays, out_ref, sems = iter(refs[:-2]), refs[-2], refs[-1]
    copies = []
    for held in sources:
        for lane, groups in held:
            for pieces in groups:
                array = next(arrays)
                for n, k in enumerate(pieces):
                    first = (lane.chunk_first + lane.first(me_ref[0], k)) * TILE
                    at = pl.ds(pl.multiple_of(first, TILE), lane.rows)
                    sem = sems.at[len(copies)]
                    piece = array.at[pl.ds(n * lane.rows, lane.rows), :]
                    copies.append(pltpu.make_async_copy(piece, out_ref.at[at, :], sem))
                    copies[-1].start()
    for copy in copies:
        copy.wait()


def assemble(lay, epoch, me, arrays):
    sources = [routes(lay, DIRECT_SPREAD, epoch, c) for c in range(lay.chunks)]
    count = sum(len(pieces) for held in sources for _, groups in held for pieces in groups)
    return pl.pallas_call(
        functools.partial(assemble_kernel, lay, sources),
        out_shape=jax.ShapeDtypeStruct((lay.items * TILE, TILE), jnp.float32),
        in_specs=[SMEM] + [VMEM] * len(arrays),
        out_specs=ANY,
        scratch_shapes=[pltpu.SemaphoreType.DMA((count,))],
        compiler_params=PARAMS,
        name="assemble",
    )(me, *arrays)


def swap(value, axis, mask):
    return lax.ppermute(value, axis, [(i, i ^ mask) for i in range(lax.axis_size(axis))])


def gather_sum(lane, direct, arrays):
    if direct:
        return [arrays[0]] + [swap(array, "replica", k) for k, array in enumerate(arrays) if k]
    parts, leave, held = [arrays[0]], arrays[1], lane.replicas
    for bit in lane.bits:
        held //= 2
        if held < lane.replicas // 2:
            half = slice(held * lane.sent, 2 * held * lane.sent)
            leave = functools.reduce(jnp.add, [part[half] for part in parts])
        parts.append(swap(leave, "replica", bit))
    return parts


def spread(lane, direct, own):
    if direct:
        return [own] + [swap(own, "replica", k) for k in range(1, lane.replicas)]
    held = own
    for bit in reversed(lane.bits[1:]):
        held = jnp.concatenate([held, swap(held, "replica", bit)], axis=0)
    return [held, swap(held, "replica", lane.bits[0])]


def steps(flip, lay, user_factors, item_factors, ratings, user_tile, item_tile, live_count):
    me = lax.axis_index("replica").astype(jnp.int32).reshape(1)
    epochs = ratings.shape[0]
    rows = user_factors
    table, low, lowt = prepare(lay, user_tile, item_tile, live_count.T, rows)
    blocks = [[[item_factors]]] * lay.chunks
    for e in range(epochs):
        last = e + 1 == epochs
        grads, parts = [], []
        for c in range(lay.chunks):
            block = [array for arrays in blocks[c] for array in arrays]
            grad, pieces = slot_terms(lay, e, c, table, me, ratings, low, lowt, block)
            grads.append(grad)
            parts.append([gather_sum(lane, DIRECT_SUM[e][c], held) for lane, held in zip(lay.lanes[e][c], pieces)])
        if last:
            (rows,) = user_step(lay, e, last, table, rows, grads)
        else:
            rows, low, lowt = user_step(lay, e, last, table, rows, grads)
        fresh = []
        for c in range(lay.chunks):
            lanes = []
            for n, lane in enumerate(lay.lanes[e][c]):
                same = len(blocks[c]) == len(lay.lanes[e][c])
                old = blocks[c][n if same else 0][0]
                own = item_step(lane, e == 0, 0 if same else lane.skip, me, old, parts[c][n])
                if not last:
                    own = swap(own, "stratum", flip)
                lanes.append(spread(lane, DIRECT_SPREAD[e][c], own))
            fresh.append(lanes)
        blocks = fresh
    arrays = [array for lanes in blocks for held in lanes for array in held]
    return rows, assemble(lay, epochs - 1, me, arrays)


def local(user_factors, item_factors, ratings, user_tile, item_tile, live_count, partner):
    users, items = user_factors.shape[0] // TILE, item_factors.shape[0] // TILE
    replicas, strata = lax.axis_size("replica"), lax.axis_size("stratum")
    lay = Layout(users, items, ratings.shape[1], replicas)
    branches = [functools.partial(steps, flip, lay) for flip in range(strata // 2, strata)]
    args = (user_factors, item_factors, ratings, user_tile, item_tile, live_count)
    return lax.switch(partner[0] - strata // 2, branches, *args)


def solution(mesh):
    split = P(("stratum", "replica"), None)
    return jax.shard_map(
        local,
        mesh=mesh,
        in_specs=(
            split,
            P("stratum", None),
            P(None, ("stratum", "replica"), None, None),
            P(None, ("stratum", "replica")),
            P(None, ("stratum", "replica")),
            P(None, ("stratum", "replica")),
            P(),
        ),
        out_specs=(split, P("stratum", None)),
        check_vma=False,
    )
```

```python
import functools

import jax
import jax.numpy as jnp
from jax import lax
from jax.experimental import pallas as pl
from jax.experimental.pallas import tpu as pltpu
from jax.sharding import PartitionSpec as P

LEARNING_RATE = 0.05
WEIGHT_DECAY = 0.05
KEEP = 1.0 - LEARNING_RATE * WEIGHT_DECAY

TILE = 128
SPLIT = (1, 1)
LANES = ((1, 1), (2, 2))
DIRECT_SUM = ((1, 1), (0, 0))
DIRECT_SPREAD = ((1, 1), (0, 0))
UNITS = 8
STEP = 2 * UNITS
AHEAD = 3
RING = 4
FIELD = 6
COUNT_ROWS = 8
VMEM_BYTES = 24 << 20
SLOT_VMEM_BYTES = 44 << 20

CONTRACT_LAST = (((1,), (1,)), ((), ()))
VMEM = pl.BlockSpec(memory_space=pltpu.VMEM)
SMEM = pl.BlockSpec(memory_space=pltpu.SMEM)
ANY = pl.BlockSpec(memory_space=pl.ANY)
PARAMS = pltpu.CompilerParams(vmem_limit_bytes=VMEM_BYTES)


def up(value, unit):
    return (value + unit - 1) // unit * unit


class Lane:
    def __init__(self, chunk_first, share, lane, lanes, replicas, turn):
        self.chunk_first, self.share, self.replicas = chunk_first, share, replicas
        self.tiles = share // lanes
        self.skip = lane * self.tiles
        self.rows = self.tiles * TILE
        self.sent = self.rows + COUNT_ROWS
        levels = replicas.bit_length() - 1
        self.bits = [1 << (lane + turn + i) % levels for i in range(levels)]

    def arrays(self, direct):
        if direct:
            return [[k] for k in range(self.replicas)]
        order = sorted(range(self.replicas), key=lambda k: [k & bit for bit in self.bits])
        return [order[: self.replicas // 2], order[self.replicas // 2 :]]

    def first(self, me, k):
        return lax.bitwise_xor(me, k) * self.share + self.skip


class Layout:
    def __init__(self, users, items, slots, replicas):
        self.users, self.items, self.slots, self.replicas = users, items, slots, replicas
        self.tiles = [items * part // sum(SPLIT) for part in SPLIT]
        self.firsts = [sum(self.tiles[:c]) for c in range(len(SPLIT))]
        self.chunks = len(SPLIT)
        self.lanes = []
        for wanted in LANES:
            self.lanes.append([])
            for c in range(self.chunks):
                share = self.tiles[c] // replicas
                lanes = wanted[c] if share % wanted[c] == 0 else 1
                self.lanes[-1].append([Lane(self.firsts[c], share, n, lanes, replicas, c) for n in range(lanes)])
        self.groups = self.chunks * users
        self.group_cols = up(self.groups + 1, 128)
        self.depth = up(slots + users, STEP) // STEP
        self.info_at = self.depth + AHEAD
        self.seen_at = self.info_at + 1
        self.count_at = self.info_at + 2
        self.table_rows = up(self.info_at + 3, 8)


ME, EPOCH, STEPS, FIRST = range(4)


def column(row, across):
    one = jnp.broadcast_to(row, (128, row.shape[1])).T
    return jnp.concatenate([one] * (across // 128), axis=1)


def low_tiles(rows, low_ref, lowt_ref, a):
    low = rows.astype(jnp.bfloat16)
    low_ref[a] = low
    lowt_ref[a] = low.T


def slot_table(lay, user, item, live):
    def iota(shape, axis):
        return lax.broadcasted_iota(jnp.int32, shape, axis)

    def total(mask, values=1):
        return jnp.sum(jnp.where(mask, values, 0), axis=0, keepdims=True)

    n, groups, users = lay.slots, lay.group_cols, lay.users
    chunk = sum((item >= first).astype(jnp.int32) for first in lay.firsts[1:]) + jnp.zeros_like(item)
    local = item - sum(jnp.where(chunk == c, first, 0) for c, first in enumerate(lay.firsts))
    group = jnp.where(live, chunk * users + user, lay.groups)
    packed = user + (local << FIELD) + (iota((1, n), 1) << 2 * FIELD)
    same = column(group, n) == group
    rank = total(same & (iota((n, n), 0) < iota((n, n), 1)))
    count = total(column(group, groups) == iota((n, groups), 1))
    padded = column((count + 1) // 2 * 2, groups)
    above, here = iota((groups, groups), 0), iota((groups, groups), 1)
    kin = above // users == here // users
    inside = total((above < here) & kin, padded)
    steps = (total(kin, padded) + STEP - 1) // STEP
    every = iota((1, groups), 1)
    base = every // users * (lay.depth * STEP) + inside
    place = rank + total(iota((groups, n), 0) == group, column(base, n))
    place = jnp.where(live, place, -1)
    spare = jnp.where((count % 2 == 1) & (every < lay.groups), base + count, -1)
    pad = sum(jnp.where(every // users == c, tiles, 0) for c, tiles in enumerate(lay.tiles))
    cols = up(lay.chunks * lay.depth * STEP, 128)
    order = total(column(place, cols) == iota((n, cols), 1), column(packed - users, cols))
    order += total(column(spare, cols) == iota((groups, cols), 1), column(every % users - users + (pad << FIELD), cols))
    order += users
    seen_user = total(column(jnp.where(live, user, -1), 128) == iota((n, 128), 1))
    seen_item = total(column(jnp.where(live, item, -1), 128) == iota((n, 128), 1))
    return order, steps, seen_user, seen_item


def prepare_kernel(lay, epochs, me_ref, user_ref, item_ref, live_ref, rows_hbm, *refs):
    tables, (low_ref, lowt_ref, rows_ref, sems) = refs[:-4], refs[-4:]
    parts = sems.shape[0]
    height = rows_ref.shape[0] // parts
    copies = []
    for p in range(parts):
        at = pl.ds(p * height, height)
        copies.append(pltpu.make_async_copy(rows_hbm.at[at, :], rows_ref.at[at, :], sems.at[p]))
        copies[-1].start()
    lane = lax.broadcasted_iota(jnp.int32, (lay.table_rows, 128), 1)
    mask = (1 << FIELD) - 1
    for e in range(epochs):
        live = lax.broadcasted_iota(jnp.int32, (1, lay.slots), 1) < live_ref[:, e : e + 1]
        order, steps, seen_user, seen_item = slot_table(lay, user_ref[e : e + 1, :], item_ref[e : e + 1, :], live)
        every = lax.broadcasted_iota(jnp.int32, steps.shape, 1)
        for c in range(lay.chunks):
            table_ref = tables[e * lay.chunks + c]
            table_ref[...] = jnp.full(table_ref.shape, lay.users, jnp.int32)
            for g in range(lay.depth):
                at = (c * lay.depth + g) * STEP
                table_ref[g : g + 1, 0:STEP] = order[:, at : at + STEP]
            packed = table_ref[...]
            user = pltpu.roll(packed & mask, STEP, 1)
            item = pltpu.roll((packed >> FIELD) & mask, 2 * STEP, 1)
            table_ref[...] = jnp.where(lane < STEP, packed >> 2 * FIELD, jnp.where(lane < 2 * STEP, user, item))
            mine = jnp.sum(jnp.where(every == c * lay.users, steps, 0), axis=1, keepdims=True)
            info = jnp.where(lane[:1] == STEPS, mine, lay.firsts[c])
            info = jnp.where(lane[:1] == ME, me_ref[0], jnp.where(lane[:1] == EPOCH, e, info))
            table_ref[lay.info_at : lay.info_at + 1, :] = info
            table_ref[lay.seen_at : lay.seen_at + 1, :] = seen_item
            table_ref[lay.count_at : lay.count_at + 1, :] = seen_user
    low_ref[lay.users] = jnp.zeros((TILE, TILE), jnp.bfloat16)
    lowt_ref[lay.users] = jnp.zeros((TILE, TILE), jnp.bfloat16)
    share = lay.users // parts
    for p in range(parts):
        copies[p].wait()

        def lower(i, _, p=p):
            a = p * share + i
            low_tiles(rows_ref[pl.ds(pl.multiple_of(a * TILE, TILE), TILE), :], low_ref, lowt_ref, a)
            return 0

        lax.fori_loop(0, share, lower, 0, unroll=4)


def low_shape(lay):
    return jax.ShapeDtypeStruct((lay.users + 1, TILE, TILE), jnp.bfloat16)


def prepare(lay, me, user_tile, item_tile, live_count, user_rows):
    epochs = user_tile.shape[0]
    parts = 4
    out = pl.pallas_call(
        functools.partial(prepare_kernel, lay, epochs),
        out_shape=[jax.ShapeDtypeStruct((lay.table_rows, 128), jnp.int32)] * (epochs * lay.chunks)
        + [low_shape(lay)] * 2,
        in_specs=[SMEM, VMEM, VMEM, VMEM, ANY],
        out_specs=[VMEM] * (epochs * lay.chunks + 2),
        scratch_shapes=[pltpu.VMEM(user_rows.shape, jnp.float32), pltpu.SemaphoreType.DMA((parts,))],
        compiler_params=PARAMS,
        name="prepare",
    )(me, user_tile, item_tile, live_count, user_rows)
    tables = [out[e * lay.chunks : (e + 1) * lay.chunks] for e in range(epochs)]
    return tables, out[-2], out[-1]


def slots_kernel(
    lay, sources, targets, tiles, table_ref, ratings_ref, low_ref, lowt_ref, *refs
):
    count_in = sum(len(arrays) for _, arrays in sources) if sources else 1
    count_out = sum(len(arrays) for _, arrays in targets)
    block_refs, refs = refs[:count_in], refs[count_in:]
    user_grad, piece_refs = refs[0], refs[1 : 1 + count_out]
    buf, sems, item_low, item_grad = refs[1 + count_out :]
    me, epoch, steps, chunk_first = [table_ref[lay.info_at, n] for n in (ME, EPOCH, STEPS, FIRST)]
    zero = jnp.zeros((TILE, TILE), jnp.float32)

    def fetch(g):
        ring = lax.bitwise_and(g, RING - 1)
        for s in range(STEP):
            slot = table_ref[g, s]
            pltpu.make_async_copy(ratings_ref.at[epoch, slot], buf.at[ring, s], sems.at[ring]).start()

    def land(g):
        ring = lax.bitwise_and(g, RING - 1)
        pltpu.make_async_copy(ratings_ref.at[epoch, pl.ds(0, STEP)], buf.at[ring], sems.at[ring]).wait()

    def fetch_first(g, _):
        fetch(g)
        return 0

    lax.fori_loop(0, AHEAD, fetch_first, 0)

    if sources:
        inputs = iter(block_refs)
        for lane, arrays in sources:
            for pieces in arrays:
                block = next(inputs)
                for n, k in enumerate(pieces):
                    first = lane.first(me, k)
                    for j in range(lane.tiles):
                        at = n * lane.rows + j * TILE
                        item_low[first + j] = block[at : at + TILE, :].astype(jnp.bfloat16)
    else:


        def lower(j, _):
            at = pl.ds(pl.multiple_of((chunk_first + j) * TILE, TILE), TILE)
            item_low[j] = block_refs[0][at, :].astype(jnp.bfloat16)
            return 0

        lax.fori_loop(0, tiles, lower, 0, unroll=4)
    item_low[tiles] = jnp.zeros((TILE, TILE), jnp.bfloat16)

    def clear_item(a, _):
        item_grad[a] = zero
        return 0

    def clear_user(a, _):
        user_grad[a] = zero
        return 0

    lax.fori_loop(0, tiles, clear_item, 0, unroll=4)
    lax.fori_loop(0, lay.users, clear_user, 0, unroll=4)

    def step(g, _):
        land(g)
        fetch(g + AHEAD)
        ring = lax.bitwise_and(g, RING - 1)
        units = []
        for n in range(UNITS):
            user = table_ref[g, STEP + 2 * n]
            items = [table_ref[g, 2 * STEP + 2 * n + s] for s in range(2)]
            right = jnp.concatenate([item_low[b] for b in items], axis=0)
            predicted = lax.dot_general(low_ref[user], right, CONTRACT_LAST, preferred_element_type=jnp.float32)
            rating = jnp.concatenate([buf[ring, 2 * n + s] for s in range(2)], axis=1)
            residual = (rating.astype(jnp.float32) - predicted).astype(jnp.bfloat16)
            units.append((user, items, right, residual))
        for user, items, right, residual in units:
            user_grad[user] += jnp.dot(residual, right, preferred_element_type=jnp.float32)
            part = jnp.dot(lowt_ref[user], residual, preferred_element_type=jnp.float32)
            for s in range(2):
                item_grad[items[s]] += part[:, s * TILE : (s + 1) * TILE]
        return 0

    lax.fori_loop(0, steps, step, 0)

    def turn(j, _):
        item_grad[j] = item_grad[j].T
        return 0

    lax.fori_loop(0, tiles, turn, 0, unroll=2)
    row = lax.broadcasted_iota(jnp.int32, (COUNT_ROWS, TILE), 0)
    outputs = iter(piece_refs)
    for lane, arrays in targets:
        for pieces in arrays:
            out = next(outputs)
            for n, k in enumerate(pieces):
                first = lane.first(me, k)
                counts = jnp.zeros((COUNT_ROWS, TILE), jnp.int32)
                for j in range(lane.tiles):
                    at = n * lane.sent + j * TILE
                    out[at : at + TILE, :] = item_grad[first + j]
                    seen = table_ref[lay.seen_at, chunk_first + first + j]
                    counts = jnp.where(row == j, seen, counts)
                at = n * lane.sent + lane.rows
                out[at : at + COUNT_ROWS, :] = counts.astype(jnp.float32)

    def drain(g, _):
        land(steps + g)
        return 0

    lax.fori_loop(0, AHEAD, drain, 0)


def routes(lay, direct, epoch, chunk):
    return [(lane, lane.arrays(direct[epoch][chunk])) for lane in lay.lanes[epoch][chunk]]


def slot_terms(lay, epoch, chunk, table, ratings, low, lowt, blocks):
    sources = routes(lay, DIRECT_SPREAD, epoch - 1, chunk) if epoch else None
    targets = routes(lay, DIRECT_SUM, epoch, chunk)
    pieces = [
        jax.ShapeDtypeStruct((len(held) * lane.sent, TILE), jnp.float32)
        for lane, arrays in targets
        for held in arrays
    ]
    user_grad = jax.ShapeDtypeStruct((lay.users + 1, TILE, TILE), jnp.float32)
    live = lay.slots // lay.chunks
    out = pl.pallas_call(
        functools.partial(slots_kernel, lay, sources, targets, lay.tiles[chunk]),
        out_shape=[user_grad] + pieces,
        in_specs=[SMEM, ANY, VMEM, VMEM] + [VMEM] * len(blocks),
        out_specs=[VMEM] * (1 + len(pieces)),
        scratch_shapes=[
            pltpu.VMEM((RING, STEP, TILE, TILE), jnp.bfloat16),
            pltpu.SemaphoreType.DMA((RING,)),
            pltpu.VMEM((lay.tiles[chunk] + 1, TILE, TILE), jnp.bfloat16),
            pltpu.VMEM((lay.tiles[chunk] + 1, TILE, TILE), jnp.float32),
        ],
        cost_estimate=pl.CostEstimate(
            flops=6 * live * TILE**3 * 4, bytes_accessed=live * TILE * TILE * 2, transcendentals=0
        ),
        compiler_params=pltpu.CompilerParams(vmem_limit_bytes=SLOT_VMEM_BYTES),
        name="slots",
    )(table, ratings, low, lowt, *blocks)
    parts = iter(out[1:])
    return out[0], [[next(parts) for _ in arrays] for _, arrays in targets]


def user_kernel(lay, last, table_ref, rows_ref, *refs):
    grads, refs = refs[: lay.chunks], refs[lay.chunks :]

    def one(a, _):
        seen = table_ref[lay.count_at, a]
        seen = jnp.maximum(jnp.broadcast_to(seen, (1, TILE)).astype(jnp.float32), 1.0)
        at = pl.ds(pl.multiple_of(a * TILE, TILE), TILE)
        grad = sum(grad_ref[a] for grad_ref in grads)
        rows = rows_ref[at, :] * KEEP + grad * (LEARNING_RATE / seen)
        refs[0][at, :] = rows
        if not last:
            low_tiles(rows, refs[1], refs[2], a)
        return 0

    lax.fori_loop(0, lay.users, one, 0, unroll=4)
    if not last:
        refs[1][lay.users] = jnp.zeros((TILE, TILE), jnp.bfloat16)
        refs[2][lay.users] = jnp.zeros((TILE, TILE), jnp.bfloat16)


def user_step(lay, last, table, rows, grads):
    out_shape = [jax.ShapeDtypeStruct(rows.shape, jnp.float32)]
    if not last:
        out_shape += [low_shape(lay)] * 2
    return pl.pallas_call(
        functools.partial(user_kernel, lay, last),
        out_shape=out_shape,
        in_specs=[SMEM] + [VMEM] * (1 + len(grads)),
        out_specs=[VMEM] * len(out_shape),
        compiler_params=PARAMS,
        name="users",
    )(table, rows, *grads)


def item_kernel(lane, whole, skip, me_ref, old_ref, *refs):
    parts, out_ref = refs[:-1], refs[-1]
    first = lane.chunk_first + lane.first(me_ref[0], 0) if whole else skip
    for j in range(lane.tiles):
        at = slice(j * TILE, (j + 1) * TILE)
        from_tile = (first + j) * TILE
        old = old_ref[pl.ds(pl.multiple_of(from_tile, TILE) if whole else from_tile, TILE), :]
        row = lane.rows + j
        seen = jnp.maximum(sum(part[row : row + 1, :] for part in parts), 1.0)
        grad = sum(part[at, :] for part in parts)
        out_ref[at, :] = old * KEEP + grad * (LEARNING_RATE / seen)


def item_step(lane, whole, skip, me, old, parts):
    return pl.pallas_call(
        functools.partial(item_kernel, lane, whole, skip),
        out_shape=jax.ShapeDtypeStruct((lane.rows, TILE), jnp.float32),
        in_specs=[SMEM] + [VMEM] * (1 + len(parts)),
        out_specs=VMEM,
        compiler_params=PARAMS,
        name="items",
    )(me, old, *parts)


def assemble_kernel(lay, sources, me_ref, *refs):
    arrays, out_ref, sems = iter(refs[:-2]), refs[-2], refs[-1]
    copies = []
    for held in sources:
        for lane, groups in held:
            for pieces in groups:
                array = next(arrays)
                for n, k in enumerate(pieces):
                    first = (lane.chunk_first + lane.first(me_ref[0], k)) * TILE
                    at = pl.ds(pl.multiple_of(first, TILE), lane.rows)
                    sem = sems.at[len(copies)]
                    piece = array.at[pl.ds(n * lane.rows, lane.rows), :]
                    copies.append(pltpu.make_async_copy(piece, out_ref.at[at, :], sem))
                    copies[-1].start()
    for copy in copies:
        copy.wait()


def assemble(lay, epoch, me, arrays):
    sources = [routes(lay, DIRECT_SPREAD, epoch, c) for c in range(lay.chunks)]
    count = sum(len(pieces) for held in sources for _, groups in held for pieces in groups)
    return pl.pallas_call(
        functools.partial(assemble_kernel, lay, sources),
        out_shape=jax.ShapeDtypeStruct((lay.items * TILE, TILE), jnp.float32),
        in_specs=[SMEM] + [VMEM] * len(arrays),
        out_specs=ANY,
        scratch_shapes=[pltpu.SemaphoreType.DMA((count,))],
        compiler_params=PARAMS,
        name="assemble",
    )(me, *arrays)


def swap(value, axis, mask):
    return lax.ppermute(value, axis, [(i, i ^ mask) for i in range(lax.axis_size(axis))])


def gather_sum(lane, direct, arrays):
    if direct:
        return [arrays[0]] + [swap(array, "replica", k) for k, array in enumerate(arrays) if k]
    parts, leave, held = [arrays[0]], arrays[1], lane.replicas
    for bit in lane.bits:
        held //= 2
        if held < lane.replicas // 2:
            half = slice(held * lane.sent, 2 * held * lane.sent)
            leave = functools.reduce(jnp.add, [part[half] for part in parts])
        parts.append(swap(leave, "replica", bit))
    return parts


def spread(lane, direct, own):
    if direct:
        return [own] + [swap(own, "replica", k) for k in range(1, lane.replicas)]
    held = own
    for bit in reversed(lane.bits[1:]):
        held = jnp.concatenate([held, swap(held, "replica", bit)], axis=0)
    return [held, swap(held, "replica", lane.bits[0])]


def steps(flip, lay, user_factors, item_factors, ratings, user_tile, item_tile, live_count):
    me = lax.axis_index("replica").astype(jnp.int32).reshape(1)
    epochs = ratings.shape[0]
    rows = user_factors
    tables, low, lowt = prepare(lay, me, user_tile, item_tile, live_count.T, rows)
    blocks = [[[item_factors]]] * lay.chunks
    for e in range(epochs):
        last = e + 1 == epochs
        grads, parts = [], []
        for c in range(lay.chunks):
            block = [array for arrays in blocks[c] for array in arrays]
            grad, pieces = slot_terms(lay, e, c, tables[e][c], ratings, low, lowt, block)
            grads.append(grad)
            parts.append([gather_sum(lane, DIRECT_SUM[e][c], held) for lane, held in zip(lay.lanes[e][c], pieces)])
        if last:
            (rows,) = user_step(lay, last, tables[e][0], rows, grads)
        else:
            rows, low, lowt = user_step(lay, last, tables[e][0], rows, grads)
        fresh = []
        for c in range(lay.chunks):
            lanes = []
            for n, lane in enumerate(lay.lanes[e][c]):
                same = len(blocks[c]) == len(lay.lanes[e][c])
                old = blocks[c][n if same else 0][0]
                own = item_step(lane, e == 0, 0 if same else lane.skip, me, old, parts[c][n])
                if not last:
                    own = swap(own, "stratum", flip)
                lanes.append(spread(lane, DIRECT_SPREAD[e][c], own))
            fresh.append(lanes)
        blocks = fresh
    arrays = [array for lanes in blocks for held in lanes for array in held]
    return rows, assemble(lay, epochs - 1, me, arrays)


def local(user_factors, item_factors, ratings, user_tile, item_tile, live_count, partner):
    users, items = user_factors.shape[0] // TILE, item_factors.shape[0] // TILE
    replicas, strata = lax.axis_size("replica"), lax.axis_size("stratum")
    lay = Layout(users, items, ratings.shape[1], replicas)
    branches = [functools.partial(steps, flip, lay) for flip in range(strata // 2, strata)]
    args = (user_factors, item_factors, ratings, user_tile, item_tile, live_count)
    return lax.switch(partner[0] - strata // 2, branches, *args)


def solution(mesh):
    split = P(("stratum", "replica"), None)
    return jax.shard_map(
        local,
        mesh=mesh,
        in_specs=(
            split,
            P("stratum", None),
            P(None, ("stratum", "replica"), None, None),
            P(None, ("stratum", "replica")),
            P(None, ("stratum", "replica")),
            P(None, ("stratum", "replica")),
            P(),
        ),
        out_specs=(split, P("stratum", None)),
        check_vma=False,
    )
```
